32 devices in a mesh: groups: 2 (over y), dp: 4 (over z), opt: 4 (over x, core).
Axes of the slice: x: 2, y: 2, z: 4, core: 2. Of those that a mesh axis runs over, the one named last changes fastest.
Arguments:
- gate_pre: bfloat16 [2048, 14336], P(('groups', 'dp'), 'opt'), parts along dimension 0, may hold values from -6 to 6
- up_pre: bfloat16 [2048, 14336], P(('groups', 'dp'), 'opt'), parts along dimension 0, may hold values from -6 to 6
- cotangent: bfloat16 [2048, 4096], P(('groups', 'dp'), 'opt'), parts along dimension 0, may hold values from -6 to 6
- down_weight: bfloat16 [4096, 14336], P('dp', 'opt'), may hold values from -0.046875 to 0.046875
- projector: bfloat16 [8192, 1024], P(('groups', 'opt')), parts along dimension 0, may hold values from -0.09375 to 0.09375
- moment_first: float32 [2048, 14336], P(('groups', 'dp'), 'opt'), parts along dimension 0, may hold values from -6 to 6
- moment_second: float32 [2048, 14336], P(('groups', 'dp'), 'opt'), parts along dimension 0, may hold values from 1.024 to 10.24
Outputs:
- gate_grad: bfloat16 [2048, 14336], P(('groups', 'dp'), 'opt'), parts along dimension 0
- up_grad: bfloat16 [2048, 14336], P(('groups', 'dp'), 'opt'), parts along dimension 0
- weight_update: bfloat16 [8192, 14336], P(('groups', 'dp'), 'opt'), parts along dimension 0
The draws below stay inside these ranges and needn't reach their ends.
There are 2 independent parts, one for each index of `groups`. The reference program is written for one: setup_inputs(seed, part) draws one part's arguments, and reference() takes and returns one part's arrays. A program takes and returns all parts, laid end to end along the dimension named above; an argument that names none is the same for every part. Nothing has to cross between parts.
All inputs are finite; a program needn't handle non-finite values.
Results may differ from the reference program's by a relative error of at most 0.006.
Values may be sent and summed in bfloat16 or wider, within the bound.
A program may use at most 192 MiB of HBM per device.

```python
import math
import jax
import jax.numpy as jnp

D = 4096
FF = 14336
R = 1024
TOKENS = 1024


def block_levels(stream_key, dims, shards, least, top_value):
    level, own = 1.0, jax.random.fold_in(stream_key, 6)
    for position, parts in shards:
        heights = jnp.exp(jax.random.uniform(jax.random.fold_in(own, position), (parts,), jnp.float32, least / len(shards), top_value / len(shards)))
        level = level * jnp.repeat(heights, dims[position] // parts).reshape([-1 if axis == position else 1 for axis in range(len(dims))])
    return level


def scatter_about(rng, dims, width, limit, split=(), dtype=jnp.bfloat16):
    entries = jax.random.normal(rng, dims, jnp.float32) * width
    if len(split) > 0:
        entries = block_levels(rng, dims, split, -0.22, 0.18) * entries
    return jnp.clip(entries, min=-limit, max=limit).astype(dtype)


def setup_inputs(seed: int = 0, part: int = 0) -> dict:
    splits = jax.random.split(jax.random.key(seed), 8)
    own_keys = jax.random.split(jax.random.fold_in(splits[7], part), 8)
    return {
        "gate_pre": scatter_about(own_keys[0], (TOKENS, FF), 1.0, 6.0, ((0, 4), (1, 4))),
        "up_pre": scatter_about(own_keys[1], (TOKENS, FF), 1.0, 6.0, ((0, 4), (1, 4))),
        "cotangent": scatter_about(own_keys[2], (TOKENS, D), 1.0, 6.0, ((0, 4), (1, 4))),
        "down_weight": scatter_about(splits[3], (D, FF), FF ** -0.5, 0.046875, ((0, 4), (1, 4))),
        "projector": scatter_about(own_keys[4], (D, R), D ** -0.5, 0.09375, ((0, 4),)),
        "moment_first": scatter_about(own_keys[5], (R, FF), (0.03 * TOKENS ** 0.5), 6.0, ((0, 4), (1, 4)), jnp.float32),
        "moment_second": jnp.clip(jnp.exp(math.log(10.24) - 2.30258502 * jax.random.uniform(own_keys[6], (R, FF), jnp.float32) ** block_levels(own_keys[6], (R, FF), ((0, 4), (1, 4)), -0.2, 0.2)), 1.024, 10.24),
    }


decay_first = 0.9
decay_second = 0.999
fix_first = 1.0 - 0.9 ** 4
fix_second = 1.0 - 0.999 ** 4
epsilon = 1e-08

def reference(gate_pre, up_pre, cotangent, down_weight, projector, moment_first, moment_second):
    gate_wide = gate_pre.astype(jnp.float32)
    up_wide = up_pre.astype(jnp.float32)
    sigmoid_gate = jax.nn.sigmoid(gate_wide)
    swish_gate = gate_wide * sigmoid_gate
    hidden = (swish_gate * up_wide).astype(jnp.bfloat16)
    hidden_grad = jnp.dot(cotangent, down_weight, preferred_element_type=jnp.float32)
    gate_grad = (hidden_grad * up_wide * sigmoid_gate * (1.0 + gate_wide * (1.0 - sigmoid_gate))).astype(jnp.bfloat16)
    up_grad = (hidden_grad * swish_gate).astype(jnp.bfloat16)
    projected = jnp.dot(cotangent, projector, preferred_element_type=jnp.float32).astype(jnp.bfloat16)
    lowrank = jnp.dot(projected.T, hidden, preferred_element_type=jnp.float32)
    first = decay_first * moment_first + (1.0 - decay_first) * lowrank
    second = decay_second * moment_second + (1.0 - decay_second) * lowrank * lowrank
    direction = (first / fix_first / (jnp.sqrt(second / fix_second) + epsilon)).astype(jnp.bfloat16)
    weight_update = jnp.dot(projector, direction, preferred_element_type=jnp.float32).astype(jnp.bfloat16)
    return (gate_grad, up_grad, weight_update)
```

```python
import functools

import jax
import jax.numpy as jnp
from jax import lax
from jax.experimental import pallas as pl
from jax.experimental.pallas import tpu as pltpu
from jax.sharding import PartitionSpec as P

decay_first = 0.9
decay_second = 0.999
fix_first = 1.0 - 0.9**4
fix_second = 1.0 - 0.999**4
epsilon = 1e-08

MESH = pl.DeviceIdType.MESH
f32 = jnp.float32
bf16 = jnp.bfloat16


def kernel(n, m, C, CA, gate, up, cot, w, proj, m1, m2, gg_out, ug_out, wu_out,
           gate_v, up_v, cot_v, w_v, proj_v, m1_v, m2_v,
           hid, hidb, dirn, cot_all, pmatch, part, precv, pown, pall, hgb, lrb, stage,
           load, out_sem, wu_sem, c1s, c1r, c2s, c2r, pas, par, pbs, pbr, pzs, pzr, pms, pmr,
           hsr, hsl, hr, lrs, lrr, hgs, hgr, dsr, dsl, dr):
    CB = C - CA
    tok, ff = gate.shape
    cw = ff // C
    feat = w.shape[0]
    rn = m1.shape[0]
    rm = part.shape[0] // m
    tq = tok // m
    d = lax.axis_index("dp")
    o = lax.axis_index("opt")
    last = n - 1

    def cols(c):
        return pl.ds(pl.multiple_of(c * cw, cw), cw)

    def peer(z, q):
        return {"dp": z, "opt": q}

    def remote(src, dst, ss, rs, dev):
        return pltpu.make_async_remote_copy(
            src_ref=src, dst_ref=dst, send_sem=ss, recv_sem=rs, device_id=dev, device_id_type=MESH
        )

    def each(count, body):
        def step(i, carry):
            body(i)
            return carry

        lax.fori_loop(0, count, step, 0)

    loads = [
        pltpu.make_async_copy(src, dst, load.at[i])
        for i, (src, dst) in enumerate(
            ((gate, gate_v), (up, up_v), (cot, cot_v), (proj, proj_v), (w, w_v), (m1, m1_v), (m2, m2_v))
        )
    ]
    for copy in loads:
        copy.start()

    barrier = pltpu.get_barrier_semaphore()

    def greet(i):
        @pl.when(i != d * m + o)
        def _():
            pl.semaphore_signal(barrier, inc=1, device_id=peer(i // m, i % m), device_id_type=MESH)

    each(n * m, greet)

    def make_hidden(c, store, place):
        g = gate_v[:, cols(c)].astype(f32)
        u = up_v[:, cols(c)].astype(f32)
        value = (g * jax.nn.sigmoid(g) * u).astype(bf16)
        if store is hid:
            hid[d, :, cols(place)] = value
        else:
            hidb[:, cols(place)] = value

    loads[0].wait()
    loads[1].wait()
    make_hidden(0, hid, 0)
    pl.semaphore_wait(barrier, n * m - 1)

    def ag_right(buf, ss, rs, j, c):
        return remote(buf(j, c), buf(j, c), ss.at[c * n + j], rs.at[c * n + j], peer(d + 1, o))

    def ag_left(buf, ss, rs, j, c):
        return remote(buf(j, c), buf(j, c), ss.at[c * n + j], rs.at[c * n + j], peer(d - 1, o))

    def hid_at(j, c):
        return hid.at[j, :, cols(c)]

    def dir_at(j, c):
        return dirn.at[pl.ds(pl.multiple_of(j * rn, rn), rn), cols(c)]

    def ag_own(buf, sr, sl, rs, c):
        @pl.when(d < last)
        def _():
            ag_right(buf, sr, rs, d, c).start()

        @pl.when(d > 0)
        def _():
            ag_left(buf, sl, rs, d, c).start()

    def ag_relay(buf, sr, sl, rs, s, count):
        def hop(i):
            h = i + 1
            c = s - h
            ok = jnp.logical_and(c >= 0, c < count)

            @pl.when(jnp.logical_and(ok, d - h >= 0))
            def _():
                ag_left(buf, sl, rs, d - h, c).wait_recv()

                @pl.when(d < last)
                def _():
                    ag_right(buf, sr, rs, d - h, c).start()

            @pl.when(jnp.logical_and(ok, d + h <= last))
            def _():
                ag_right(buf, sr, rs, d + h, c).wait_recv()

                @pl.when(d > 0)
                def _():
                    ag_left(buf, sl, rs, d + h, c).start()

        each(n - 1, hop)

    def ag_drain(buf, sr, sl, rs, count):
        def chunk(c):
            def source(j):
                @pl.when(jnp.logical_and(d < last, j <= d))
                def _():
                    ag_right(buf, sr, rs, j, c).wait_send()

                @pl.when(jnp.logical_and(d > 0, j >= d))
                def _():
                    ag_left(buf, sl, rs, j, c).wait_send()

            each(n, source)

        each(count, chunk)

    def rs_right(buf, ss, rs, t, c):
        return remote(buf.at[t, :, cols(c)], buf.at[t, :, cols(c)], ss.at[c * n + t],
                      rs.at[c * (n + 1) + t], peer(d + 1, o))

    def rs_left(buf, ss, rs, t, c):
        slot = jnp.where(t == d - 1, n, t)
        return remote(buf.at[t, :, cols(c)], buf.at[slot, :, cols(c)], ss.at[c * n + t],
                      rs.at[c * (n + 1) + slot], peer(d - 1, o))

    def rs_arrived_left(buf, ss, rs, slot, c):
        remote(buf.at[slot, :, cols(c)], buf.at[slot, :, cols(c)], ss.at[c * n],
               rs.at[c * (n + 1) + slot], peer(d - 1, o)).wait_recv()

    def rs_arrived_right(buf, ss, rs, slot, c):
        remote(buf.at[slot, :, cols(c)], buf.at[slot, :, cols(c)], ss.at[c * n],
               rs.at[c * (n + 1) + slot], peer(d + 1, o)).wait_recv()

    def rs_step(buf, ss, rs, s, count, term):
        cr = s - d
        cl = s - (last - d)

        def hop(k):
            t = last - k

            @pl.when(jnp.logical_and(jnp.logical_and(cr >= 0, cr < count), t > d))
            def _():
                value = term(t, cr)

                @pl.when(d > 0)
                def _():
                    rs_arrived_left(buf, ss, rs, t, cr)
                    buf[t, :, cols(cr)] = (buf[t, :, cols(cr)].astype(f32) + value).astype(bf16)

                @pl.when(d == 0)
                def _():
                    buf[t, :, cols(cr)] = value.astype(bf16)

                rs_right(buf, ss, rs, t, cr).start()

            @pl.when(jnp.logical_and(jnp.logical_and(cl >= 0, cl < count), k < d))
            def _():
                value = term(k, cl)

                @pl.when(d < last)
                def _():
                    rs_arrived_right(buf, ss, rs, k, cl)
                    buf[k, :, cols(cl)] = (buf[k, :, cols(cl)].astype(f32) + value).astype(bf16)

                @pl.when(d == last)
                def _():
                    buf[k, :, cols(cl)] = value.astype(bf16)

                rs_left(buf, ss, rs, k, cl).start()

        each(n - 1, hop)

    def rs_take(buf, ss, rs, c, value):
        @pl.when(d > 0)
        def _():
            rs_arrived_left(buf, ss, rs, d, c)

        @pl.when(d == 0)
        def _():
            buf[d, :, cols(c)] = jnp.zeros(value.shape, bf16)

        @pl.when(d < last)
        def _():
            rs_arrived_right(buf, ss, rs, n, c)

        @pl.when(d == last)
        def _():
            buf[n, :, cols(c)] = jnp.zeros(value.shape, bf16)

        return value + buf[d, :, cols(c)].astype(f32) + buf[n, :, cols(c)].astype(f32)

    def rs_drain(buf, ss, rs, count):
        def chunk(c):
            def dest(t):
                @pl.when(t > d)
                def _():
                    rs_right(buf, ss, rs, t, c).wait_send()

                @pl.when(t < d)
                def _():
                    rs_left(buf, ss, rs, t, c).wait_send()

            each(n, dest)

        each(count, chunk)

    ag_own(hid_at, hsr, hsl, hr, 0)

    loads[2].wait()
    loads[3].wait()

    for q in range(m):
        part[q * rm:(q + 1) * rm, :] = lax.dot_general(
            proj_v[:, q * rm:(q + 1) * rm], cot_v[...], (((0,), (1,)), ((), ())),
            preferred_element_type=f32,
        )

    def part_rows(q):
        return part.at[pl.ds(pl.multiple_of(q * rm, rm), rm), :]

    def pa_send(q):
        return remote(part_rows(q), precv.at[o], pas.at[q], par.at[o], peer(d, q))

    def pa_recv(q):
        return remote(part_rows(q), precv.at[q], pas.at[q], par.at[q], peer(d, q))

    def c1_send(q):
        return remote(cot_v.at[pl.ds(pl.multiple_of(q * tq, tq), tq), :], cot_all.at[q, d],
                      c1s.at[q], c1r.at[d], peer(o, q))

    def others(body):
        def one(q):
            @pl.when(q != o)
            def _():
                body(q)

        each(m, one)

    others(lambda q: pa_send(q).start())

    def is_self(q):
        return jnp.logical_and(o == d, q == o)

    def c1_start(q):
        @pl.when(jnp.logical_not(is_self(q)))
        def _():
            c1_send(q).start()

    each(m, c1_start)

    @pl.when(o == d)
    def _():
        cot_all[o, d] = cot_v[pl.ds(pl.multiple_of(o * tq, tq), tq), :]

    def rest(c):
        make_hidden(c + 1, hid, c + 1)

    each(CA - 1, rest)

    def restb(c):
        make_hidden(c + CA, hidb, c)

    each(CB, restb)

    precv[o] = part[pl.ds(pl.multiple_of(o * rm, rm), rm), :]
    others(lambda q: pa_recv(q).wait_recv())
    total = precv[0]
    for q in range(1, m):
        total = total + precv[q]
    mine = total.astype(bf16)
    pown[o] = mine

    @pl.when(o == d)
    def _():
        pall[d] = mine

    def pb_send(q):
        return remote(pown.at[o], pown.at[o], pbs.at[q], pbr.at[o], peer(d, q))

    def pb_recv(q):
        return remote(pown.at[q], pown.at[q], pbs.at[q], pbr.at[q], peer(d, q))

    def pz_send(q):
        return remote(pown.at[o], pall.at[d], pzs.at[q], pzr.at[d], peer(o, q))

    others(lambda q: pb_send(q).start())

    def pz_start(q):
        @pl.when(jnp.logical_not(is_self(q)))
        def _():
            pz_send(q).start()

    each(m, pz_start)
    others(lambda q: pb_recv(q).wait_recv())

    def lr_term(t, c):
        return jnp.dot(pown[t], hidb[:, cols(c)], preferred_element_type=f32)

    def c2_send(q):
        return remote(cot_all.at[o], cot_all.at[o], c2s.at[q], c2r.at[o], peer(d, q))

    def c2_recv(q):
        return remote(cot_all.at[q], cot_all.at[q], c2s.at[q], c2r.at[q], peer(d, q))

    def from_layers(wait):
        def one(z):
            @pl.when(jnp.logical_or(z != d, o != d))
            def _():
                wait(z)

        each(n, one)

    def pm_send(q):
        return remote(proj_v, pmatch, pms.at[q], pmr, peer(d, q))

    def phase1(s):
        @pl.when(jnp.logical_and(s > 0, s < CA))
        def _():
            ag_own(hid_at, hsr, hsl, hr, s)

        rs_step(lrb, lrs, lrr, s, CB, lr_term)
        ag_relay(hid_at, hsr, hsl, hr, s, CA)

        @pl.when(s == 0)
        def _():
            from_layers(lambda z: remote(cot_all.at[o, z], cot_all.at[o, z], c1s.at[0], c1r.at[z],
                                         peer(d, lax.rem(o + 1, m))).wait_recv())
            others(lambda q: c2_send(q).start())

            @pl.when(o == d)
            def _():
                others(lambda q: pm_send(q).start())
                pmatch[...] = proj_v[...]

    each(max(CA + n - 1, CB + n - 1), phase1)

    from_layers(lambda z: remote(pall.at[z], pall.at[z], pzs.at[0], pzr.at[z],
                                 peer(d, lax.rem(o + 1, m))).wait_recv())
    others(lambda q: c2_recv(q).wait_recv())
    for i in (4, 5, 6):
        loads[i].wait()

    @pl.when(o != d)
    def _():
        remote(proj_v, pmatch, pms.at[0], pmr, peer(d, d)).wait_recv()

    def hg_term(t, c):
        rows = cot_all[:, pl.ds(t, 1)].reshape(tok, feat)
        return jnp.dot(rows, w_v[:, cols(c)], preferred_element_type=f32)

    def adam(lowrank, c):
        first = decay_first * m1_v[:, cols(c)] + (1.0 - decay_first) * lowrank
        second = decay_second * m2_v[:, cols(c)] + (1.0 - decay_second) * lowrank * lowrank
        value = (first / fix_first / (jnp.sqrt(second / fix_second) + epsilon)).astype(bf16)
        dirn[pl.ds(pl.multiple_of(d * rn, rn), rn), cols(c)] = value

    def out_copies(c):
        return (
            pltpu.make_async_copy(gate_v.at[:, cols(c)], gg_out.at[:, cols(c)], out_sem.at[2 * c]),
            pltpu.make_async_copy(up_v.at[:, cols(c)], ug_out.at[:, cols(c)], out_sem.at[2 * c + 1]),
        )

    def wu_copy(c):
        slot = lax.rem(c, 2)
        return pltpu.make_async_copy(stage.at[slot], wu_out.at[:, cols(c)], wu_sem.at[slot])

    rows_step = min(256, feat)

    def phase2(s):
        rs_step(hgb, hgs, hgr, s, C, hg_term)

        @pl.when(s < CA)
        def _():
            def add(j, acc):
                return acc + jnp.dot(pall[j], hid[j, :, cols(s)], preferred_element_type=f32)

            adam(lax.fori_loop(0, n, add, jnp.zeros((rn, cw), f32)), s)

        @pl.when(jnp.logical_and(s >= CA, s < C))
        def _():
            c = s - CA
            adam(rs_take(lrb, lrs, lrr, c, lr_term(d, c)), s)

        @pl.when(s < C)
        def _():
            ag_own(dir_at, dsr, dsl, dr, s)

        ag_relay(dir_at, dsr, dsl, dr, s, C)

        c = s - last

        @pl.when(c >= 0)
        def _():
            g = gate_v[:, cols(c)].astype(f32)
            u = up_v[:, cols(c)].astype(f32)
            sig = jax.nn.sigmoid(g)
            grad = rs_take(hgb, hgs, hgr, c, hg_term(d, c))
            gate_v[:, cols(c)] = (grad * u * sig * (1.0 + g * (1.0 - sig))).astype(bf16)
            up_v[:, cols(c)] = (grad * (g * sig)).astype(bf16)
            for copy in out_copies(c):
                copy.start()

            @pl.when(c >= 2)
            def _():
                wu_copy(c - 2).wait()

            slot = lax.rem(c, 2)

            def tile(i):
                rows = pl.ds(pl.multiple_of(i * rows_step, rows_step), rows_step)
                stage[slot, rows, :] = jnp.dot(
                    pmatch[rows, :], dirn[:, cols(c)], preferred_element_type=f32
                ).astype(bf16)

            each(feat // rows_step, tile)
            wu_copy(c).start()

    each(C + n - 1, phase2)

    ag_drain(hid_at, hsr, hsl, hr, CA)
    rs_drain(lrb, lrs, lrr, CB)
    rs_drain(hgb, hgs, hgr, C)
    ag_drain(dir_at, dsr, dsl, dr, C)
    others(lambda q: pa_send(q).wait_send())
    others(lambda q: pb_send(q).wait_send())
    others(lambda q: c2_send(q).wait_send())

    def tail(q):
        @pl.when(jnp.logical_not(is_self(q)))
        def _():
            c1_send(q).wait_send()
            pz_send(q).wait_send()

    each(m, tail)

    @pl.when(o == d)
    def _():
        others(lambda q: pm_send(q).wait_send())

    def finish(c):
        for copy in out_copies(c):
            copy.wait()

    each(C, finish)
    wu_copy(C - 2).wait()
    wu_copy(C - 1).wait()


def per_device(n, m, gate_pre, up_pre, cotangent, down_weight, projector, moment_first, moment_second):
    tok, ff = gate_pre.shape
    feat, rank = projector.shape
    rn = moment_first.shape[0]
    C, CA = 7, 4
    CB = C - CA
    cw = ff // C
    dma = pltpu.SemaphoreType.DMA
    vmem = pltpu.VMEM
    return pl.pallas_call(
        functools.partial(kernel, n, m, C, CA),
        out_shape=(
            jax.ShapeDtypeStruct((tok, ff), bf16),
            jax.ShapeDtypeStruct((tok, ff), bf16),
            jax.ShapeDtypeStruct((feat, ff), bf16),
        ),
        in_specs=[pl.BlockSpec(memory_space=pl.ANY)] * 7,
        out_specs=[pl.BlockSpec(memory_space=pl.ANY)] * 3,
        scratch_shapes=[
            vmem((tok, ff), bf16), vmem((tok, ff), bf16), vmem(cotangent.shape, bf16),
            vmem((feat, ff), bf16), vmem((feat, rank), bf16),
            vmem((rn, ff), f32), vmem((rn, ff), f32),
            vmem((n, tok, CA * cw), bf16), vmem((tok, CB * cw), bf16), vmem((rank, ff), bf16),
            vmem((m, n, tok // m, feat), bf16), vmem((feat, rank), bf16),
            vmem((rank, tok), f32), vmem((m, rank // m, tok), f32),
            vmem((m, rank // m, tok), bf16), vmem((n, rn, tok), bf16),
            vmem((n + 1, tok, ff), bf16), vmem((n + 1, rn, CB * cw), bf16),
            vmem((2, feat, cw), bf16),
            dma((7,)), dma((2 * C,)), dma((2,)),
            dma((m,)), dma((n,)), dma((m,)), dma((m,)), dma((m,)), dma((m,)), dma((m,)), dma((m,)),
            dma((m,)), dma((n,)), dma((m,)), dma,
            dma((CA * n,)), dma((CA * n,)), dma((CA * n,)),
            dma((CB * n,)), dma((CB * (n + 1),)), dma((C * n,)), dma((C * (n + 1),)),
            dma((C * n,)), dma((C * n,)), dma((C * n,)),
        ],
        compiler_params=pltpu.CompilerParams(
            collective_id=0, has_side_effects=True, vmem_limit_bytes=62 * 1024 * 1024
        ),
    )(gate_pre, up_pre, cotangent, down_weight, projector, moment_first, moment_second)


def solution(mesh):
    in_specs = (
        P(("groups", "dp"), "opt"),
        P(("groups", "dp"), "opt"),
        P(("groups", "dp"), "opt"),
        P("dp", "opt"),
        P(("groups", "opt"), None),
        P(("groups", "dp"), "opt"),
        P(("groups", "dp"), "opt"),
    )
    out_specs = (P(("groups", "dp"), "opt"), P(("groups", "dp"), "opt"), P(("groups", "dp"), "opt"))
    return jax.shard_map(
        functools.partial(per_device, mesh.shape["dp"], mesh.shape["opt"]),
        mesh=mesh, in_specs=in_specs, out_specs=out_specs, check_vma=False,
    )
```

```python
import functools

import jax
import jax.numpy as jnp
from jax import lax
from jax.experimental import pallas as pl
from jax.experimental.pallas import tpu as pltpu
from jax.sharding import PartitionSpec as P

decay_first = 0.9
decay_second = 0.999
fix_first = 1.0 - 0.9**4
fix_second = 1.0 - 0.999**4
epsilon = 1e-08

MESH = pl.DeviceIdType.MESH
f32 = jnp.float32
bf16 = jnp.bfloat16


def kernel(n, m, C, CA, lag, sp, gate, up, cot, w, proj, m1, m2, gg_out, ug_out, wu_out,
           gate_v, up_v, cot_v, w_v, proj_v, m1_v, m2_v,
           hid, hidb, dirn, cot_all, pmatch, part, precv, pown, pall, hgb, lrb, stage,
           load, out_sem, wu_sem, c1s, c1r, c2s, c2r, pas, par, pbs, pbr, pzs, pzr, p3s, p3r, pms, pmr,
           hsr, hsl, hr, lrs, lrr, hgs, hgr, dsr, dsl, dr):
    CB = C - CA
    tok, ff = gate.shape
    cw = ff // C
    feat = w.shape[0]
    rn = m1.shape[0]
    rm = part.shape[0] // m
    tq = tok // m
    d = lax.axis_index("dp")
    o = lax.axis_index("opt")
    last = n - 1

    def cols(c):
        return pl.ds(pl.multiple_of(c * cw, cw), cw)

    def peer(z, q):
        return {"dp": z, "opt": q}

    def remote(src, dst, ss, rs, dev):
        return pltpu.make_async_remote_copy(
            src_ref=src, dst_ref=dst, send_sem=ss, recv_sem=rs, device_id=dev, device_id_type=MESH
        )

    def each(count, body):
        def step(i, carry):
            body(i)
            return carry

        lax.fori_loop(0, count, step, 0)

    loads = [
        pltpu.make_async_copy(src, dst, load.at[i])
        for i, (src, dst) in enumerate(
            ((gate, gate_v), (up, up_v), (cot, cot_v), (proj, proj_v), (w, w_v), (m1, m1_v), (m2, m2_v))
        )
    ]
    for copy in loads:
        copy.start()

    barrier = pltpu.get_barrier_semaphore()

    def greet(i):
        @pl.when(i != d * m + o)
        def _():
            pl.semaphore_signal(barrier, inc=1, device_id=peer(i // m, i % m), device_id_type=MESH)

    each(n * m, greet)

    def make_hidden(c, store, place):
        g = gate_v[:, cols(c)].astype(f32)
        u = up_v[:, cols(c)].astype(f32)
        value = (g * jax.nn.sigmoid(g) * u).astype(bf16)
        if store is hid:
            hid[d, :, cols(place)] = value
        else:
            hidb[:, cols(place)] = value

    loads[0].wait()
    loads[1].wait()
    make_hidden(0, hid, 0)
    pl.semaphore_wait(barrier, n * m - 1)

    def ag_right(buf, ss, rs, j, c):
        return remote(buf(j, c), buf(j, c), ss.at[c * n + j], rs.at[c * n + j], peer(d + 1, o))

    def ag_left(buf, ss, rs, j, c):
        return remote(buf(j, c), buf(j, c), ss.at[c * n + j], rs.at[c * n + j], peer(d - 1, o))

    def hid_at(j, c):
        return hid.at[j, :, cols(c)]

    def dir_at(j, c):
        return dirn.at[pl.ds(pl.multiple_of(j * rn, rn), rn), cols(c)]

    def ag_own(buf, sr, sl, rs, c):
        @pl.when(d < last)
        def _():
            ag_right(buf, sr, rs, d, c).start()

        @pl.when(d > 0)
        def _():
            ag_left(buf, sl, rs, d, c).start()

    def ag_relay(buf, sr, sl, rs, s, count):
        def hop(i):
            h = i + 1
            c = s - lag * h
            ok = jnp.logical_and(c >= 0, c < count)

            @pl.when(jnp.logical_and(ok, d - h >= 0))
            def _():
                ag_left(buf, sl, rs, d - h, c).wait_recv()

                @pl.when(d < last)
                def _():
                    ag_right(buf, sr, rs, d - h, c).start()

            @pl.when(jnp.logical_and(ok, d + h <= last))
            def _():
                ag_right(buf, sr, rs, d + h, c).wait_recv()

                @pl.when(d > 0)
                def _():
                    ag_left(buf, sl, rs, d + h, c).start()

        each(n - 1, hop)

    def ag_drain(buf, sr, sl, rs, count):
        def chunk(c):
            def source(j):
                @pl.when(jnp.logical_and(d < last, j <= d))
                def _():
                    ag_right(buf, sr, rs, j, c).wait_send()

                @pl.when(jnp.logical_and(d > 0, j >= d))
                def _():
                    ag_left(buf, sl, rs, j, c).wait_send()

            each(n, source)

        each(count, chunk)

    def rs_right(buf, ss, rs, t, c):
        return remote(buf.at[t, :, cols(c)], buf.at[t, :, cols(c)], ss.at[c * n + t],
                      rs.at[c * (n + 1) + t], peer(d + 1, o))

    def rs_left(buf, ss, rs, t, c):
        slot = jnp.where(t == d - 1, n, t)
        return remote(buf.at[t, :, cols(c)], buf.at[slot, :, cols(c)], ss.at[c * n + t],
                      rs.at[c * (n + 1) + slot], peer(d - 1, o))

    def rs_arrived_left(buf, ss, rs, slot, c):
        remote(buf.at[slot, :, cols(c)], buf.at[slot, :, cols(c)], ss.at[c * n],
               rs.at[c * (n + 1) + slot], peer(d - 1, o)).wait_recv()

    def rs_arrived_right(buf, ss, rs, slot, c):
        remote(buf.at[slot, :, cols(c)], buf.at[slot, :, cols(c)], ss.at[c * n],
               rs.at[c * (n + 1) + slot], peer(d + 1, o)).wait_recv()

    def rs_step(buf, ss, rs, s, count, term):
        cr = s - lag * d
        cl = s - lag * (last - d)

        def hop(k):
            t = last - k

            @pl.when(jnp.logical_and(jnp.logical_and(cr >= 0, cr < count), t > d))
            def _():
                value = term(t, cr)

                @pl.when(d > 0)
                def _():
                    rs_arrived_left(buf, ss, rs, t, cr)
                    buf[t, :, cols(cr)] = (buf[t, :, cols(cr)].astype(f32) + value).astype(bf16)

                @pl.when(d == 0)
                def _():
                    buf[t, :, cols(cr)] = value.astype(bf16)

                rs_right(buf, ss, rs, t, cr).start()

            @pl.when(jnp.logical_and(jnp.logical_and(cl >= 0, cl < count), k < d))
            def _():
                value = term(k, cl)

                @pl.when(d < last)
                def _():
                    rs_arrived_right(buf, ss, rs, k, cl)
                    buf[k, :, cols(cl)] = (buf[k, :, cols(cl)].astype(f32) + value).astype(bf16)

                @pl.when(d == last)
                def _():
                    buf[k, :, cols(cl)] = value.astype(bf16)

                rs_left(buf, ss, rs, k, cl).start()

        each(n - 1, hop)

    def rs_take(buf, ss, rs, c, value):
        @pl.when(d > 0)
        def _():
            rs_arrived_left(buf, ss, rs, d, c)

        @pl.when(d == 0)
        def _():
            buf[d, :, cols(c)] = jnp.zeros(value.shape, bf16)

        @pl.when(d < last)
        def _():
            rs_arrived_right(buf, ss, rs, n, c)

        @pl.when(d == last)
        def _():
            buf[n, :, cols(c)] = jnp.zeros(value.shape, bf16)

        return value + buf[d, :, cols(c)].astype(f32) + buf[n, :, cols(c)].astype(f32)

    def rs_drain(buf, ss, rs, count):
        def chunk(c):
            def dest(t):
                @pl.when(t > d)
                def _():
                    rs_right(buf, ss, rs, t, c).wait_send()

                @pl.when(t < d)
                def _():
                    rs_left(buf, ss, rs, t, c).wait_send()

            each(n, dest)

        each(count, chunk)

    ag_own(hid_at, hsr, hsl, hr, 0)

    loads[2].wait()
    loads[3].wait()

    for q in range(m):
        part[q * rm:(q + 1) * rm, :] = lax.dot_general(
            proj_v[:, q * rm:(q + 1) * rm], cot_v[...], (((0,), (1,)), ((), ())),
            preferred_element_type=f32,
        )

    def part_rows(q):
        return part.at[pl.ds(pl.multiple_of(q * rm, rm), rm), :]

    def pa_send(q):
        return remote(part_rows(q), precv.at[o], pas.at[q], par.at[o], peer(d, q))

    def pa_recv(q):
        return remote(part_rows(q), precv.at[q], pas.at[q], par.at[q], peer(d, q))

    def c1_send(q):
        return remote(cot_v.at[pl.ds(pl.multiple_of(q * tq, tq), tq), :], cot_all.at[q, d],
                      c1s.at[q], c1r.at[d], peer(o, q))

    def others(body):
        def one(q):
            @pl.when(q != o)
            def _():
                body(q)

        each(m, one)

    others(lambda q: pa_send(q).start())

    def is_self(q):
        return jnp.logical_and(o == d, q == o)

    def c1_start(q):
        @pl.when(jnp.logical_not(is_self(q)))
        def _():
            c1_send(q).start()

    each(m, c1_start)

    @pl.when(o == d)
    def _():
        cot_all[o, d] = cot_v[pl.ds(pl.multiple_of(o * tq, tq), tq), :]

    def rest(c):
        make_hidden(c + 1, hid, c + 1)

    each(CA - 1, rest)

    def restb(c):
        make_hidden(c + CA, hidb, c)

    each(CB, restb)

    precv[o] = part[pl.ds(pl.multiple_of(o * rm, rm), rm), :]
    others(lambda q: pa_recv(q).wait_recv())
    total = precv[0]
    for q in range(1, m):
        total = total + precv[q]
    mine = total.astype(bf16)
    pown[o] = mine

    pq = rm // sp

    def piece(q):
        return pl.ds(pl.multiple_of(q * pq, pq), pq)

    @pl.when(jnp.logical_and(o == d, o < sp))
    def _():
        pall[d, piece(o), :] = pown[o, piece(o), :]

    def pb_send(q):
        return remote(pown.at[o], pown.at[o], pbs.at[q], pbr.at[o], peer(d, q))

    def pb_recv(q):
        return remote(pown.at[q], pown.at[q], pbs.at[q], pbr.at[q], peer(d, q))

    def pz_send(q):
        return remote(pown.at[o, piece(q), :], pall.at[d, piece(q), :], pzs.at[q], pzr.at[d], peer(o, q))

    def p3_send(q):
        return remote(pall.at[:, piece(o), :], pall.at[:, piece(o), :], p3s.at[q], p3r.at[o], peer(d, q))

    def p3_recv(q):
        return remote(pall.at[:, piece(q), :], pall.at[:, piece(q), :], p3s.at[q], p3r.at[q], peer(d, q))

    others(lambda q: pb_send(q).start())

    def pz_start(q):
        @pl.when(jnp.logical_not(is_self(q)))
        def _():
            pz_send(q).start()

    each(sp, pz_start)
    others(lambda q: pb_recv(q).wait_recv())

    def lr_term(t, c):
        return jnp.dot(pown[t], hidb[:, cols(c)], preferred_element_type=f32)

    def c2_send(q):
        return remote(cot_all.at[o], cot_all.at[o], c2s.at[q], c2r.at[o], peer(d, q))

    def c2_recv(q):
        return remote(cot_all.at[q], cot_all.at[q], c2s.at[q], c2r.at[q], peer(d, q))

    def from_layers(wait):
        def one(z):
            @pl.when(jnp.logical_or(z != d, o != d))
            def _():
                wait(z)

        each(n, one)

    def pm_send(q):
        return remote(proj_v, pmatch, pms.at[q], pmr, peer(d, q))

    def phase1(s):
        @pl.when(jnp.logical_and(s > 0, s < CA))
        def _():
            ag_own(hid_at, hsr, hsl, hr, s)

        rs_step(lrb, lrs, lrr, s, CB, lr_term)
        ag_relay(hid_at, hsr, hsl, hr, s, CA)

        @pl.when(s == 2)
        def _():
            from_layers(lambda z: remote(cot_all.at[o, z], cot_all.at[o, z], c1s.at[0], c1r.at[z],
                                         peer(d, lax.rem(o + 1, m))).wait_recv())
            others(lambda q: c2_send(q).start())

            @pl.when(o < sp)
            def _():
                from_layers(lambda z: remote(pall.at[z, piece(o), :], pall.at[z, piece(o), :], pzs.at[0],
                                             pzr.at[z], peer(d, lax.rem(o + 1, m))).wait_recv())
                others(lambda q: p3_send(q).start())

            @pl.when(o == d)
            def _():
                others(lambda q: pm_send(q).start())
                pmatch[...] = proj_v[...]

    each(max(CA, CB) + lag * last, phase1)

    def p3_wait(q):
        @pl.when(q < sp)
        def _():
            p3_recv(q).wait_recv()

    others(p3_wait)
    others(lambda q: c2_recv(q).wait_recv())
    for i in (4, 5, 6):
        loads[i].wait()

    @pl.when(o != d)
    def _():
        remote(proj_v, pmatch, pms.at[0], pmr, peer(d, d)).wait_recv()

    def hg_term(t, c):
        rows = cot_all[:, pl.ds(t, 1)].reshape(tok, feat)
        return jnp.dot(rows, w_v[:, cols(c)], preferred_element_type=f32)

    def adam(lowrank, c):
        first = decay_first * m1_v[:, cols(c)] + (1.0 - decay_first) * lowrank
        second = decay_second * m2_v[:, cols(c)] + (1.0 - decay_second) * lowrank * lowrank
        value = (first / fix_first / (jnp.sqrt(second / fix_second) + epsilon)).astype(bf16)
        dirn[pl.ds(pl.multiple_of(d * rn, rn), rn), cols(c)] = value

    def out_copies(c):
        return (
            pltpu.make_async_copy(gate_v.at[:, cols(c)], gg_out.at[:, cols(c)], out_sem.at[2 * c]),
            pltpu.make_async_copy(up_v.at[:, cols(c)], ug_out.at[:, cols(c)], out_sem.at[2 * c + 1]),
        )

    def wu_copy(c):
        slot = lax.rem(c, 2)
        return pltpu.make_async_copy(stage.at[slot], wu_out.at[:, cols(c)], wu_sem.at[slot])

    rows_step = min(256, feat)

    def phase2(s):
        rs_step(hgb, hgs, hgr, s, C, hg_term)

        @pl.when(s < CA)
        def _():
            def add(j, acc):
                return acc + jnp.dot(pall[j], hid[j, :, cols(s)], preferred_element_type=f32)

            adam(lax.fori_loop(0, n, add, jnp.zeros((rn, cw), f32)), s)

        @pl.when(jnp.logical_and(s >= CA, s < C))
        def _():
            c = s - CA
            adam(rs_take(lrb, lrs, lrr, c, lr_term(d, c)), s)

        @pl.when(s < C)
        def _():
            ag_own(dir_at, dsr, dsl, dr, s)

        ag_relay(dir_at, dsr, dsl, dr, s, C)

        c = s - lag * last

        @pl.when(c >= 0)
        def _():
            g = gate_v[:, cols(c)].astype(f32)
            u = up_v[:, cols(c)].astype(f32)
            sig = jax.nn.sigmoid(g)
            grad = rs_take(hgb, hgs, hgr, c, hg_term(d, c))
            gate_v[:, cols(c)] = (grad * u * sig * (1.0 + g * (1.0 - sig))).astype(bf16)
            up_v[:, cols(c)] = (grad * (g * sig)).astype(bf16)
            for copy in out_copies(c):
                copy.start()

            @pl.when(c >= 2)
            def _():
                wu_copy(c - 2).wait()

            slot = lax.rem(c, 2)

            def tile(i):
                rows = pl.ds(pl.multiple_of(i * rows_step, rows_step), rows_step)
                stage[slot, rows, :] = jnp.dot(
                    pmatch[rows, :], dirn[:, cols(c)], preferred_element_type=f32
                ).astype(bf16)

            each(feat // rows_step, tile)
            wu_copy(c).start()

    each(C + lag * last, phase2)

    ag_drain(hid_at, hsr, hsl, hr, CA)
    rs_drain(lrb, lrs, lrr, CB)
    rs_drain(hgb, hgs, hgr, C)
    ag_drain(dir_at, dsr, dsl, dr, C)
    others(lambda q: pa_send(q).wait_send())
    others(lambda q: pb_send(q).wait_send())
    others(lambda q: c2_send(q).wait_send())

    def tail(q):
        @pl.when(jnp.logical_not(is_self(q)))
        def _():
            c1_send(q).wait_send()

            @pl.when(q < sp)
            def _():
                pz_send(q).wait_send()

    each(m, tail)

    @pl.when(o < sp)
    def _():
        others(lambda q: p3_send(q).wait_send())

    @pl.when(o == d)
    def _():
        others(lambda q: pm_send(q).wait_send())

    def finish(c):
        for copy in out_copies(c):
            copy.wait()

    each(C, finish)
    wu_copy(C - 2).wait()
    wu_copy(C - 1).wait()


def per_device(n, m, gate_pre, up_pre, cotangent, down_weight, projector, moment_first, moment_second):
    tok, ff = gate_pre.shape
    feat, rank = projector.shape
    rn = moment_first.shape[0]
    C, CA, lag = (14, 7, 1) if ff % (14 * 128) == 0 else (7, 4, 1)
    sp = min(m, rank // m // 16)
    CB = C - CA
    cw = ff // C
    dma = pltpu.SemaphoreType.DMA
    vmem = pltpu.VMEM
    return pl.pallas_call(
        functools.partial(kernel, n, m, C, CA, lag, sp),
        out_shape=(
            jax.ShapeDtypeStruct((tok, ff), bf16),
            jax.ShapeDtypeStruct((tok, ff), bf16),
            jax.ShapeDtypeStruct((feat, ff), bf16),
        ),
        in_specs=[pl.BlockSpec(memory_space=pl.ANY)] * 7,
        out_specs=[pl.BlockSpec(memory_space=pl.ANY)] * 3,
        scratch_shapes=[
            vmem((tok, ff), bf16), vmem((tok, ff), bf16), vmem(cotangent.shape, bf16),
            vmem((feat, ff), bf16), vmem((feat, rank), bf16),
            vmem((rn, ff), f32), vmem((rn, ff), f32),
            vmem((n, tok, CA * cw), bf16), vmem((tok, CB * cw), bf16), vmem((rank, ff), bf16),
            vmem((m, n, tok // m, feat), bf16), vmem((feat, rank), bf16),
            vmem((rank, tok), f32), vmem((m, rank // m, tok), f32),
            vmem((m, rank // m, tok), bf16), vmem((n, rn, tok), bf16),
            vmem((n + 1, tok, ff), bf16), vmem((n + 1, rn, CB * cw), bf16),
            vmem((2, feat, cw), bf16),
            dma((7,)), dma((2 * C,)), dma((2,)),
            dma((m,)), dma((n,)), dma((m,)), dma((m,)), dma((m,)), dma((m,)), dma((m,)), dma((m,)),
            dma((m,)), dma((n,)), dma((m,)), dma((m,)), dma((m,)), dma,
            dma((CA * n,)), dma((CA * n,)), dma((CA * n,)),
            dma((CB * n,)), dma((CB * (n + 1),)), dma((C * n,)), dma((C * (n + 1),)),
            dma((C * n,)), dma((C * n,)), dma((C * n,)),
        ],
        compiler_params=pltpu.CompilerParams(
            collective_id=0, has_side_effects=True, vmem_limit_bytes=62 * 1024 * 1024
        ),
    )(gate_pre, up_pre, cotangent, down_weight, projector, moment_first, moment_second)


def solution(mesh):
    in_specs = (
        P(("groups", "dp"), "opt"),
        P(("groups", "dp"), "opt"),
        P(("groups", "dp"), "opt"),
        P("dp", "opt"),
        P(("groups", "opt"), None),
        P(("groups", "dp"), "opt"),
        P(("groups", "dp"), "opt"),
    )
    out_specs = (P(("groups", "dp"), "opt"), P(("groups", "dp"), "opt"), P(("groups", "dp"), "opt"))
    return jax.shard_map(
        functools.partial(per_device, mesh.shape["dp"], mesh.shape["opt"]),
        mesh=mesh, in_specs=in_specs, out_specs=out_specs, check_vma=False,
    )
```

```python
import functools

import jax
import jax.numpy as jnp
from jax import lax
from jax.experimental import pallas as pl
from jax.experimental.pallas import tpu as pltpu
from jax.sharding import PartitionSpec as P

decay_first = 0.9
decay_second = 0.999
fix_first = 1.0 - 0.9**4
fix_second = 1.0 - 0.999**4
epsilon = 1e-08

MESH = pl.DeviceIdType.MESH
f32 = jnp.float32
bf16 = jnp.bfloat16


def kernel(n, m, C, CA, lag, sp, gate, up, cot, w, proj, m1, m2, gg_out, ug_out, wu_out,
           gate_v, up_v, cot_v, w_v, proj_v, m1_v, m2_v,
           hid, hidb, dirn, cot_all, pmatch, part, precv, pown, pall, hgb, lrb, stage,
           load, out_sem, wu_sem, c1s, c1r, c2s, c2r, pas, par, pbs, pbr, pzs, pzr, p3s, p3r, pms, pmr,
           hsr, hsl, hr, lrs, lrr, hgs, hgr, dsr, dsl, dr):
    CB = C - CA
    tok, ff = gate.shape
    cw = ff // C
    feat = w.shape[0]
    rn = m1.shape[0]
    rm = part.shape[0] // m
    tq = tok // m
    d = lax.axis_index("dp")
    o = lax.axis_index("opt")
    last = n - 1

    def cols(c):
        return pl.ds(pl.multiple_of(c * cw, cw), cw)

    def peer(z, q):
        return {"dp": z, "opt": q}

    def remote(src, dst, ss, rs, dev):
        return pltpu.make_async_remote_copy(
            src_ref=src, dst_ref=dst, send_sem=ss, recv_sem=rs, device_id=dev, device_id_type=MESH
        )

    def each(count, body):
        def step(i, carry):
            body(i)
            return carry

        lax.fori_loop(0, count, step, 0)

    loads = [
        pltpu.make_async_copy(src, dst, load.at[i])
        for i, (src, dst) in enumerate(
            ((gate, gate_v), (up, up_v), (cot, cot_v), (proj, proj_v), (w, w_v), (m1, m1_v), (m2, m2_v))
        )
    ]
    for copy in loads:
        copy.start()

    barrier = pltpu.get_barrier_semaphore()

    def greet(i):
        @pl.when(i != d * m + o)
        def _():
            pl.semaphore_signal(barrier, inc=1, device_id=peer(i // m, i % m), device_id_type=MESH)

    each(n * m, greet)

    def make_hidden(c, store, place):
        g = gate_v[:, cols(c)].astype(f32)
        u = up_v[:, cols(c)].astype(f32)
        value = (g * jax.nn.sigmoid(g) * u).astype(bf16)
        if store is hid:
            hid[d, :, cols(place)] = value
        else:
            hidb[:, cols(place)] = value

    loads[0].wait()
    loads[1].wait()
    make_hidden(0, hid, 0)
    pl.semaphore_wait(barrier, n * m - 1)

    def ag_right(buf, ss, rs, j, c):
        return remote(buf(j, c), buf(j, c), ss.at[c * n + j], rs.at[c * n + j], peer(d + 1, o))

    def ag_left(buf, ss, rs, j, c):
        return remote(buf(j, c), buf(j, c), ss.at[c * n + j], rs.at[c * n + j], peer(d - 1, o))

    def hid_at(j, c):
        return hid.at[j, :, cols(c)]

    def dir_at(j, c):
        return dirn.at[pl.ds(pl.multiple_of(j * rn, rn), rn), cols(c)]

    def ag_own(buf, sr, sl, rs, c):
        @pl.when(d < last)
        def _():
            ag_right(buf, sr, rs, d, c).start()

        @pl.when(d > 0)
        def _():
            ag_left(buf, sl, rs, d, c).start()

    def ag_relay(buf, sr, sl, rs, s, count):
        def hop(i):
            h = i + 1
            c = s - lag * h
            ok = jnp.logical_and(c >= 0, c < count)

            @pl.when(jnp.logical_and(ok, d - h >= 0))
            def _():
                ag_left(buf, sl, rs, d - h, c).wait_recv()

                @pl.when(d < last)
                def _():
                    ag_right(buf, sr, rs, d - h, c).start()

            @pl.when(jnp.logical_and(ok, d + h <= last))
            def _():
                ag_right(buf, sr, rs, d + h, c).wait_recv()

                @pl.when(d > 0)
                def _():
                    ag_left(buf, sl, rs, d + h, c).start()

        each(n - 1, hop)

    def ag_drain(buf, sr, sl, rs, count):
        def chunk(c):
            def source(j):
                @pl.when(jnp.logical_and(d < last, j <= d))
                def _():
                    ag_right(buf, sr, rs, j, c).wait_send()

                @pl.when(jnp.logical_and(d > 0, j >= d))
                def _():
                    ag_left(buf, sl, rs, j, c).wait_send()

            each(n, source)

        each(count, chunk)

    def rs_right(buf, ss, rs, t, c):
        return remote(buf.at[t, :, cols(c)], buf.at[t, :, cols(c)], ss.at[c * n + t],
                      rs.at[c * (n + 1) + t], peer(d + 1, o))

    def rs_left(buf, ss, rs, t, c):
        slot = jnp.where(t == d - 1, n, t)
        return remote(buf.at[t, :, cols(c)], buf.at[slot, :, cols(c)], ss.at[c * n + t],
                      rs.at[c * (n + 1) + slot], peer(d - 1, o))

    def rs_arrived_left(buf, ss, rs, slot, c):
        remote(buf.at[slot, :, cols(c)], buf.at[slot, :, cols(c)], ss.at[c * n],
               rs.at[c * (n + 1) + slot], peer(d - 1, o)).wait_recv()

    def rs_arrived_right(buf, ss, rs, slot, c):
        remote(buf.at[slot, :, cols(c)], buf.at[slot, :, cols(c)], ss.at[c * n],
               rs.at[c * (n + 1) + slot], peer(d + 1, o)).wait_recv()

    def rs_step(buf, ss, rs, s, count, term):
        cr = s - lag * d
        cl = s - lag * (last - d)

        def hop(k):
            t = last - k

            @pl.when(jnp.logical_and(jnp.logical_and(cr >= 0, cr < count), t > d))
            def _():
                value = term(t, cr)

                @pl.when(d > 0)
                def _():
                    rs_arrived_left(buf, ss, rs, t, cr)
                    buf[t, :, cols(cr)] = (buf[t, :, cols(cr)].astype(f32) + value).astype(bf16)

                @pl.when(d == 0)
                def _():
                    buf[t, :, cols(cr)] = value.astype(bf16)

                rs_right(buf, ss, rs, t, cr).start()

            @pl.when(jnp.logical_and(jnp.logical_and(cl >= 0, cl < count), k < d))
            def _():
                value = term(k, cl)

                @pl.when(d < last)
                def _():
                    rs_arrived_right(buf, ss, rs, k, cl)
                    buf[k, :, cols(cl)] = (buf[k, :, cols(cl)].astype(f32) + value).astype(bf16)

                @pl.when(d == last)
                def _():
                    buf[k, :, cols(cl)] = value.astype(bf16)

                rs_left(buf, ss, rs, k, cl).start()

        each(n - 1, hop)

    def rs_take(buf, ss, rs, c, value):
        @pl.when(d > 0)
        def _():
            rs_arrived_left(buf, ss, rs, d, c)

        @pl.when(d == 0)
        def _():
            buf[d, :, cols(c)] = jnp.zeros(value.shape, bf16)

        @pl.when(d < last)
        def _():
            rs_arrived_right(buf, ss, rs, n, c)

        @pl.when(d == last)
        def _():
            buf[n, :, cols(c)] = jnp.zeros(value.shape, bf16)

        return value + buf[d, :, cols(c)].astype(f32) + buf[n, :, cols(c)].astype(f32)

    def rs_drain(buf, ss, rs, count):
        def chunk(c):
            def dest(t):
                @pl.when(t > d)
                def _():
                    rs_right(buf, ss, rs, t, c).wait_send()

                @pl.when(t < d)
                def _():
                    rs_left(buf, ss, rs, t, c).wait_send()

            each(n, dest)

        each(count, chunk)

    ag_own(hid_at, hsr, hsl, hr, 0)

    loads[2].wait()
    loads[3].wait()

    for q in range(m):
        part[q * rm:(q + 1) * rm, :] = lax.dot_general(
            proj_v[:, q * rm:(q + 1) * rm], cot_v[...], (((0,), (1,)), ((), ())),
            preferred_element_type=f32,
        )

    def part_rows(q):
        return part.at[pl.ds(pl.multiple_of(q * rm, rm), rm), :]

    def pa_send(q):
        return remote(part_rows(q), precv.at[o], pas.at[q], par.at[o], peer(d, q))

    def pa_recv(q):
        return remote(part_rows(q), precv.at[q], pas.at[q], par.at[q], peer(d, q))

    def c1_send(q):
        return remote(cot_v.at[pl.ds(pl.multiple_of(q * tq, tq), tq), :], cot_all.at[q, d],
                      c1s.at[q], c1r.at[d], peer(o, q))

    def others(body):
        def one(q):
            @pl.when(q != o)
            def _():
                body(q)

        each(m, one)

    others(lambda q: pa_send(q).start())

    def is_self(q):
        return jnp.logical_and(o == d, q == o)

    def c1_start(q):
        @pl.when(jnp.logical_not(is_self(q)))
        def _():
            c1_send(q).start()

    each(m, c1_start)

    @pl.when(o == d)
    def _():
        cot_all[o, d] = cot_v[pl.ds(pl.multiple_of(o * tq, tq), tq), :]

    def rest(c):
        make_hidden(c + 1, hid, c + 1)

    each(CA - 1, rest)

    def restb(c):
        make_hidden(c + CA, hidb, c)

    each(CB, restb)

    precv[o] = part[pl.ds(pl.multiple_of(o * rm, rm), rm), :]
    others(lambda q: pa_recv(q).wait_recv())
    total = precv[0]
    for q in range(1, m):
        total = total + precv[q]
    mine = total.astype(bf16)
    pown[o] = mine

    pq = rm // sp

    def piece(q):
        return pl.ds(pl.multiple_of(q * pq, pq), pq)

    @pl.when(jnp.logical_and(o == d, o < sp))
    def _():
        pall[d, piece(o), :] = pown[o, piece(o), :]

    def pb_send(q):
        return remote(pown.at[o], pown.at[o], pbs.at[q], pbr.at[o], peer(d, q))

    def pb_recv(q):
        return remote(pown.at[q], pown.at[q], pbs.at[q], pbr.at[q], peer(d, q))

    def pz_send(q):
        return remote(pown.at[o, piece(q), :], pall.at[d, piece(q), :], pzs.at[q], pzr.at[d], peer(o, q))

    def p3_send(q):
        return remote(pall.at[:, piece(o), :], pall.at[:, piece(o), :], p3s.at[q], p3r.at[o], peer(d, q))

    def p3_recv(q):
        return remote(pall.at[:, piece(q), :], pall.at[:, piece(q), :], p3s.at[q], p3r.at[q], peer(d, q))

    others(lambda q: pb_send(q).start())

    def pz_start(q):
        @pl.when(jnp.logical_not(is_self(q)))
        def _():
            pz_send(q).start()

    each(sp, pz_start)
    others(lambda q: pb_recv(q).wait_recv())

    def lr_term(t, c):
        return jnp.dot(pown[t], hidb[:, cols(c)], preferred_element_type=f32)

    def c2_send(q):
        return remote(cot_all.at[o], cot_all.at[o], c2s.at[q], c2r.at[o], peer(d, q))

    def c2_recv(q):
        return remote(cot_all.at[q], cot_all.at[q], c2s.at[q], c2r.at[q], peer(d, q))

    def from_layers(wait):
        def one(z):
            @pl.when(jnp.logical_or(z != d, o != d))
            def _():
                wait(z)

        each(n, one)

    def pm_send(q):
        return remote(proj_v, pmatch, pms.at[q], pmr, peer(d, q))

    def phase1(s):
        @pl.when(jnp.logical_and(s > 0, s < CA))
        def _():
            ag_own(hid_at, hsr, hsl, hr, s)

        rs_step(lrb, lrs, lrr, s, CB, lr_term)
        ag_relay(hid_at, hsr, hsl, hr, s, CA)

        @pl.when(s == 2)
        def _():
            from_layers(lambda z: remote(cot_all.at[o, z], cot_all.at[o, z], c1s.at[0], c1r.at[z],
                                         peer(d, lax.rem(o + 1, m))).wait_recv())
            others(lambda q: c2_send(q).start())

            @pl.when(o < sp)
            def _():
                from_layers(lambda z: remote(pall.at[z, piece(o), :], pall.at[z, piece(o), :], pzs.at[0],
                                             pzr.at[z], peer(d, lax.rem(o + 1, m))).wait_recv())
                others(lambda q: p3_send(q).start())

            @pl.when(o == d)
            def _():
                others(lambda q: pm_send(q).start())
                pmatch[...] = proj_v[...]

    ahead = max(CA, lag * last)
    steps1 = max(CA, CB) + lag * last
    each(ahead, phase1)

    def p3_wait(q):
        @pl.when(q < sp)
        def _():
            p3_recv(q).wait_recv()

    others(p3_wait)
    others(lambda q: c2_recv(q).wait_recv())
    for i in (4, 5, 6):
        loads[i].wait()

    @pl.when(o != d)
    def _():
        remote(proj_v, pmatch, pms.at[0], pmr, peer(d, d)).wait_recv()

    def hg_term(t, c):
        rows = cot_all[:, pl.ds(t, 1)].reshape(tok, feat)
        return jnp.dot(rows, w_v[:, cols(c)], preferred_element_type=f32)

    def adam(lowrank, c):
        first = decay_first * m1_v[:, cols(c)] + (1.0 - decay_first) * lowrank
        second = decay_second * m2_v[:, cols(c)] + (1.0 - decay_second) * lowrank * lowrank
        value = (first / fix_first / (jnp.sqrt(second / fix_second) + epsilon)).astype(bf16)
        dirn[pl.ds(pl.multiple_of(d * rn, rn), rn), cols(c)] = value

    def out_copies(c):
        return (
            pltpu.make_async_copy(gate_v.at[:, cols(c)], gg_out.at[:, cols(c)], out_sem.at[2 * c]),
            pltpu.make_async_copy(up_v.at[:, cols(c)], ug_out.at[:, cols(c)], out_sem.at[2 * c + 1]),
        )

    def wu_copy(c):
        slot = lax.rem(c, 2)
        return pltpu.make_async_copy(stage.at[slot], wu_out.at[:, cols(c)], wu_sem.at[slot])

    rows_step = min(256, feat)

    def phase2(s):
        @pl.when(s < CA)
        def _():
            def add(j, acc):
                return acc + jnp.dot(pall[j], hid[j, :, cols(s)], preferred_element_type=f32)

            adam(lax.fori_loop(0, n, add, jnp.zeros((rn, cw), f32)), s)

        @pl.when(jnp.logical_and(s >= CA, s < C))
        def _():
            c = s - CA
            adam(rs_take(lrb, lrs, lrr, c, lr_term(d, c)), s)

        @pl.when(s < C)
        def _():
            ag_own(dir_at, dsr, dsl, dr, s)

        rs_step(hgb, hgs, hgr, s, C, hg_term)
        ag_relay(dir_at, dsr, dsl, dr, s, C)

        c = s - lag * last

        @pl.when(c >= 0)
        def _():
            g = gate_v[:, cols(c)].astype(f32)
            u = up_v[:, cols(c)].astype(f32)
            sig = jax.nn.sigmoid(g)
            grad = rs_take(hgb, hgs, hgr, c, hg_term(d, c))
            gate_v[:, cols(c)] = (grad * u * sig * (1.0 + g * (1.0 - sig))).astype(bf16)
            up_v[:, cols(c)] = (grad * (g * sig)).astype(bf16)
            for copy in out_copies(c):
                copy.start()

            @pl.when(c >= 2)
            def _():
                wu_copy(c - 2).wait()

            slot = lax.rem(c, 2)

            def tile(i):
                rows = pl.ds(pl.multiple_of(i * rows_step, rows_step), rows_step)
                stage[slot, rows, :] = jnp.dot(
                    pmatch[rows, :], dirn[:, cols(c)], preferred_element_type=f32
                ).astype(bf16)

            each(feat // rows_step, tile)
            wu_copy(c).start()

    def both(i):
        @pl.when(i + ahead < steps1)
        def _():
            phase1(i + ahead)

        phase2(i)

    each(max(C + lag * last, steps1 - ahead), both)

    ag_drain(hid_at, hsr, hsl, hr, CA)
    rs_drain(lrb, lrs, lrr, CB)
    rs_drain(hgb, hgs, hgr, C)
    ag_drain(dir_at, dsr, dsl, dr, C)
    others(lambda q: pa_send(q).wait_send())
    others(lambda q: pb_send(q).wait_send())
    others(lambda q: c2_send(q).wait_send())

    def tail(q):
        @pl.when(jnp.logical_not(is_self(q)))
        def _():
            c1_send(q).wait_send()

            @pl.when(q < sp)
            def _():
                pz_send(q).wait_send()

    each(m, tail)

    @pl.when(o < sp)
    def _():
        others(lambda q: p3_send(q).wait_send())

    @pl.when(o == d)
    def _():
        others(lambda q: pm_send(q).wait_send())

    def finish(c):
        for copy in out_copies(c):
            copy.wait()

    each(C, finish)
    wu_copy(C - 2).wait()
    wu_copy(C - 1).wait()


def per_device(n, m, gate_pre, up_pre, cotangent, down_weight, projector, moment_first, moment_second):
    tok, ff = gate_pre.shape
    feat, rank = projector.shape
    rn = moment_first.shape[0]
    C, CA, lag = (14, 7, 1) if ff % (14 * 128) == 0 else (7, 4, 1)
    sp = min(m, rank // m // 16)
    CB = C - CA
    cw = ff // C
    dma = pltpu.SemaphoreType.DMA
    vmem = pltpu.VMEM
    return pl.pallas_call(
        functools.partial(kernel, n, m, C, CA, lag, sp),
        out_shape=(
            jax.ShapeDtypeStruct((tok, ff), bf16),
            jax.ShapeDtypeStruct((tok, ff), bf16),
            jax.ShapeDtypeStruct((feat, ff), bf16),
        ),
        in_specs=[pl.BlockSpec(memory_space=pl.ANY)] * 7,
        out_specs=[pl.BlockSpec(memory_space=pl.ANY)] * 3,
        scratch_shapes=[
            vmem((tok, ff), bf16), vmem((tok, ff), bf16), vmem(cotangent.shape, bf16),
            vmem((feat, ff), bf16), vmem((feat, rank), bf16),
            vmem((rn, ff), f32), vmem((rn, ff), f32),
            vmem((n, tok, CA * cw), bf16), vmem((tok, CB * cw), bf16), vmem((rank, ff), bf16),
            vmem((m, n, tok // m, feat), bf16), vmem((feat, rank), bf16),
            vmem((rank, tok), f32), vmem((m, rank // m, tok), f32),
            vmem((m, rank // m, tok), bf16), vmem((n, rn, tok), bf16),
            vmem((n + 1, tok, ff), bf16), vmem((n + 1, rn, CB * cw), bf16),
            vmem((2, feat, cw), bf16),
            dma((7,)), dma((2 * C,)), dma((2,)),
            dma((m,)), dma((n,)), dma((m,)), dma((m,)), dma((m,)), dma((m,)), dma((m,)), dma((m,)),
            dma((m,)), dma((n,)), dma((m,)), dma((m,)), dma((m,)), dma,
            dma((CA * n,)), dma((CA * n,)), dma((CA * n,)),
            dma((CB * n,)), dma((CB * (n + 1),)), dma((C * n,)), dma((C * (n + 1),)),
            dma((C * n,)), dma((C * n,)), dma((C * n,)),
        ],
        compiler_params=pltpu.CompilerParams(
            collective_id=0, has_side_effects=True, vmem_limit_bytes=62 * 1024 * 1024
        ),
    )(gate_pre, up_pre, cotangent, down_weight, projector, moment_first, moment_second)


def solution(mesh):
    in_specs = (
        P(("groups", "dp"), "opt"),
        P(("groups", "dp"), "opt"),
        P(("groups", "dp"), "opt"),
        P("dp", "opt"),
        P(("groups", "opt"), None),
        P(("groups", "dp"), "opt"),
        P(("groups", "dp"), "opt"),
    )
    out_specs = (P(("groups", "dp"), "opt"), P(("groups", "dp"), "opt"), P(("groups", "dp"), "opt"))
    return jax.shard_map(
        functools.partial(per_device, mesh.shape["dp"], mesh.shape["opt"]),
        mesh=mesh, in_specs=in_specs, out_specs=out_specs, check_vma=False,
    )
```

```python
import functools

import jax
import jax.numpy as jnp
from jax import lax
from jax.experimental import pallas as pl
from jax.experimental.pallas import tpu as pltpu
from jax.sharding import PartitionSpec as P

decay_first = 0.9
decay_second = 0.999
fix_first = 1.0 - 0.9**4
fix_second = 1.0 - 0.999**4
epsilon = 1e-08

MESH = pl.DeviceIdType.MESH
f32 = jnp.float32
bf16 = jnp.bfloat16


def kernel(n, m, C, CA, lag, sp, gate, up, cot, w, proj, m1, m2, gg_out, ug_out, wu_out,
           gate_v, up_v, cot_v, w_v, proj_v, m1_v, m2_v,
           hid, hidb, dirn, cot_all, pmatch, part, precv, pown, pall, hgb, lrb, stage,
           load, out_sem, wu_sem, c1s, c1r, c2s, c2r, pas, par, pbs, pbr, pzs, pzr, p3s, p3r, pms, pmr,
           hsr, hsl, hr, lrs, lrr, hgs, hgr, dsr, dsl, dr):
    CB = C - CA
    tok, ff = gate.shape
    cw = ff // C
    feat = w.shape[0]
    rn = m1.shape[0]
    rm = part.shape[0] // m
    tq = tok // m
    d = lax.axis_index("dp")
    o = lax.axis_index("opt")
    last = n - 1

    def cols(c):
        return pl.ds(pl.multiple_of(c * cw, cw), cw)

    def peer(z, q):
        return {"dp": z, "opt": q}

    def remote(src, dst, ss, rs, dev):
        return pltpu.make_async_remote_copy(
            src_ref=src, dst_ref=dst, send_sem=ss, recv_sem=rs, device_id=dev, device_id_type=MESH
        )

    def each(count, body):
        def step(i, carry):
            body(i)
            return carry

        lax.fori_loop(0, count, step, 0)

    loads = [
        pltpu.make_async_copy(src, dst, load.at[i])
        for i, (src, dst) in enumerate(
            ((gate, gate_v), (up, up_v), (cot, cot_v), (proj, proj_v), (w, w_v), (m1, m1_v), (m2, m2_v))
        )
    ]
    for copy in loads:
        copy.start()

    barrier = pltpu.get_barrier_semaphore()

    def greet(i):
        @pl.when(i != d * m + o)
        def _():
            pl.semaphore_signal(barrier, inc=1, device_id=peer(i // m, i % m), device_id_type=MESH)

    each(n * m, greet)

    def make_hidden(c, store, place):
        g = gate_v[:, cols(c)].astype(f32)
        u = up_v[:, cols(c)].astype(f32)
        value = (g * jax.nn.sigmoid(g) * u).astype(bf16)
        if store is hid:
            hid[d, :, cols(place)] = value
        else:
            hidb[:, cols(place)] = value

    loads[0].wait()
    loads[1].wait()
    make_hidden(0, hid, 0)
    pl.semaphore_wait(barrier, n * m - 1)

    def ag_right(buf, ss, rs, j, c):
        return remote(buf(j, c), buf(j, c), ss.at[c * n + j], rs.at[c * n + j], peer(d + 1, o))

    def ag_left(buf, ss, rs, j, c):
        return remote(buf(j, c), buf(j, c), ss.at[c * n + j], rs.at[c * n + j], peer(d - 1, o))

    def hid_at(j, c):
        return hid.at[j, :, cols(c)]

    def dir_at(j, c):
        return dirn.at[pl.ds(pl.multiple_of(j * rn, rn), rn), cols(c)]

    def ag_own(buf, sr, sl, rs, c):
        @pl.when(d < last)
        def _():
            ag_right(buf, sr, rs, d, c).start()

        @pl.when(d > 0)
        def _():
            ag_left(buf, sl, rs, d, c).start()

    def ag_relay(buf, sr, sl, rs, s, count):
        def hop(i):
            h = i + 1
            c = s - lag * h
            ok = jnp.logical_and(c >= 0, c < count)

            @pl.when(jnp.logical_and(ok, d - h >= 0))
            def _():
                ag_left(buf, sl, rs, d - h, c).wait_recv()

                @pl.when(d < last)
                def _():
                    ag_right(buf, sr, rs, d - h, c).start()

            @pl.when(jnp.logical_and(ok, d + h <= last))
            def _():
                ag_right(buf, sr, rs, d + h, c).wait_recv()

                @pl.when(d > 0)
                def _():
                    ag_left(buf, sl, rs, d + h, c).start()

        each(n - 1, hop)

    def ag_drain(buf, sr, sl, rs, count):
        def chunk(c):
            def source(j):
                @pl.when(jnp.logical_and(d < last, j <= d))
                def _():
                    ag_right(buf, sr, rs, j, c).wait_send()

                @pl.when(jnp.logical_and(d > 0, j >= d))
                def _():
                    ag_left(buf, sl, rs, j, c).wait_send()

            each(n, source)

        each(count, chunk)

    def rs_right(buf, ss, rs, t, c):
        return remote(buf.at[t, :, cols(c)], buf.at[t, :, cols(c)], ss.at[c * n + t],
                      rs.at[c * (n + 1) + t], peer(d + 1, o))

    def rs_left(buf, ss, rs, t, c):
        slot = jnp.where(t == d - 1, n, t)
        return remote(buf.at[t, :, cols(c)], buf.at[slot, :, cols(c)], ss.at[c * n + t],
                      rs.at[c * (n + 1) + slot], peer(d - 1, o))

    def rs_arrived_left(buf, ss, rs, slot, c):
        remote(buf.at[slot, :, cols(c)], buf.at[slot, :, cols(c)], ss.at[c * n],
               rs.at[c * (n + 1) + slot], peer(d - 1, o)).wait_recv()

    def rs_arrived_right(buf, ss, rs, slot, c):
        remote(buf.at[slot, :, cols(c)], buf.at[slot, :, cols(c)], ss.at[c * n],
               rs.at[c * (n + 1) + slot], peer(d + 1, o)).wait_recv()

    def rs_step(buf, ss, rs, s, count, term):
        cr = s - lag * d
        cl = s - lag * (last - d)

        def hop(k):
            t = last - k

            @pl.when(jnp.logical_and(jnp.logical_and(cr >= 0, cr < count), t > d))
            def _():
                value = term(t, cr)

                @pl.when(d > 0)
                def _():
                    rs_arrived_left(buf, ss, rs, t, cr)
                    buf[t, :, cols(cr)] = (buf[t, :, cols(cr)].astype(f32) + value).astype(bf16)

                @pl.when(d == 0)
                def _():
                    buf[t, :, cols(cr)] = value.astype(bf16)

                rs_right(buf, ss, rs, t, cr).start()

            @pl.when(jnp.logical_and(jnp.logical_and(cl >= 0, cl < count), k < d))
            def _():
                value = term(k, cl)

                @pl.when(d < last)
                def _():
                    rs_arrived_right(buf, ss, rs, k, cl)
                    buf[k, :, cols(cl)] = (buf[k, :, cols(cl)].astype(f32) + value).astype(bf16)

                @pl.when(d == last)
                def _():
                    buf[k, :, cols(cl)] = value.astype(bf16)

                rs_left(buf, ss, rs, k, cl).start()

        each(n - 1, hop)

    def rs_take(buf, ss, rs, c, value):
        @pl.when(d > 0)
        def _():
            rs_arrived_left(buf, ss, rs, d, c)

        @pl.when(d == 0)
        def _():
            buf[d, :, cols(c)] = jnp.zeros(value.shape, bf16)

        @pl.when(d < last)
        def _():
            rs_arrived_right(buf, ss, rs, n, c)

        @pl.when(d == last)
        def _():
            buf[n, :, cols(c)] = jnp.zeros(value.shape, bf16)

        return value + buf[d, :, cols(c)].astype(f32) + buf[n, :, cols(c)].astype(f32)

    def rs_drain(buf, ss, rs, count):
        def chunk(c):
            def dest(t):
                @pl.when(t > d)
                def _():
                    rs_right(buf, ss, rs, t, c).wait_send()

                @pl.when(t < d)
                def _():
                    rs_left(buf, ss, rs, t, c).wait_send()

            each(n, dest)

        each(count, chunk)

    ag_own(hid_at, hsr, hsl, hr, 0)

    loads[2].wait()
    loads[3].wait()

    for q in range(m):
        part[q * rm:(q + 1) * rm, :] = lax.dot_general(
            proj_v[:, q * rm:(q + 1) * rm], cot_v[...], (((0,), (1,)), ((), ())),
            preferred_element_type=f32,
        )

    def part_rows(q):
        return part.at[pl.ds(pl.multiple_of(q * rm, rm), rm), :]

    def pa_send(q):
        return remote(part_rows(q), precv.at[o], pas.at[q], par.at[o], peer(d, q))

    def pa_recv(q):
        return remote(part_rows(q), precv.at[q], pas.at[q], par.at[q], peer(d, q))

    def c1_send(q):
        return remote(cot_v.at[pl.ds(pl.multiple_of(q * tq, tq), tq), :], cot_all.at[q, d],
                      c1s.at[q], c1r.at[d], peer(o, q))

    def others(body):
        def one(q):
            @pl.when(q != o)
            def _():
                body(q)

        each(m, one)

    others(lambda q: pa_send(q).start())

    def is_self(q):
        return jnp.logical_and(o == d, q == o)

    def c1_start(q):
        @pl.when(jnp.logical_not(is_self(q)))
        def _():
            c1_send(q).start()

    each(m, c1_start)

    @pl.when(o == d)
    def _():
        cot_all[o, d] = cot_v[pl.ds(pl.multiple_of(o * tq, tq), tq), :]

    def rest(c):
        make_hidden(c + 1, hid, c + 1)

    each(CA - 1, rest)

    def restb(c):
        make_hidden(c + CA, hidb, c)

    each(CB, restb)

    precv[o] = part[pl.ds(pl.multiple_of(o * rm, rm), rm), :]
    others(lambda q: pa_recv(q).wait_recv())
    total = precv[0]
    for q in range(1, m):
        total = total + precv[q]
    mine = total.astype(bf16)
    pown[o] = mine

    pq = rm // sp

    def piece(q):
        return pl.ds(pl.multiple_of(q * pq, pq), pq)

    @pl.when(jnp.logical_and(o == d, o < sp))
    def _():
        pall[d, piece(o), :] = pown[o, piece(o), :]

    def pb_send(q):
        return remote(pown.at[o], pown.at[o], pbs.at[q], pbr.at[o], peer(d, q))

    def pb_recv(q):
        return remote(pown.at[q], pown.at[q], pbs.at[q], pbr.at[q], peer(d, q))

    def pz_send(q):
        return remote(pown.at[o, piece(q), :], pall.at[d, piece(q), :], pzs.at[q], pzr.at[d], peer(o, q))

    def p3_send(q):
        return remote(pall.at[:, piece(o), :], pall.at[:, piece(o), :], p3s.at[q], p3r.at[o], peer(d, q))

    def p3_recv(q):
        return remote(pall.at[:, piece(q), :], pall.at[:, piece(q), :], p3s.at[q], p3r.at[q], peer(d, q))

    others(lambda q: pb_send(q).start())

    def pz_start(q):
        @pl.when(jnp.logical_not(is_self(q)))
        def _():
            pz_send(q).start()

    each(sp, pz_start)
    others(lambda q: pb_recv(q).wait_recv())

    def lr_term(t, c):
        return jnp.dot(pown[t], hidb[:, cols(c)], preferred_element_type=f32)

    def c2_send(q):
        return remote(cot_all.at[o], cot_all.at[o], c2s.at[q], c2r.at[o], peer(d, q))

    def c2_recv(q):
        return remote(cot_all.at[q], cot_all.at[q], c2s.at[q], c2r.at[q], peer(d, q))

    def from_layers(wait):
        def one(z):
            @pl.when(jnp.logical_or(z != d, o != d))
            def _():
                wait(z)

        each(n, one)

    def pm_send(q):
        return remote(proj_v, pmatch, pms.at[q], pmr, peer(d, q))

    def phase1(s):
        @pl.when(jnp.logical_and(s > 0, s < CA))
        def _():
            ag_own(hid_at, hsr, hsl, hr, s)

        rs_step(lrb, lrs, lrr, s, CB, lr_term)
        ag_relay(hid_at, hsr, hsl, hr, s, CA)

        @pl.when(s == 2)
        def _():
            from_layers(lambda z: remote(cot_all.at[o, z], cot_all.at[o, z], c1s.at[0], c1r.at[z],
                                         peer(d, lax.rem(o + 1, m))).wait_recv())
            others(lambda q: c2_send(q).start())

            @pl.when(o < sp)
            def _():
                from_layers(lambda z: remote(pall.at[z, piece(o), :], pall.at[z, piece(o), :], pzs.at[0],
                                             pzr.at[z], peer(d, lax.rem(o + 1, m))).wait_recv())
                others(lambda q: p3_send(q).start())

            @pl.when(o == d)
            def _():
                others(lambda q: pm_send(q).start())
                pmatch[...] = proj_v[...]

    ahead = max(CA, lag * last)
    steps1 = max(CA, CB) + lag * last
    each(ahead, phase1)

    def p3_wait(q):
        @pl.when(q < sp)
        def _():
            p3_recv(q).wait_recv()

    others(p3_wait)
    others(lambda q: c2_recv(q).wait_recv())
    for i in (4, 5, 6):
        loads[i].wait()

    @pl.when(o != d)
    def _():
        remote(proj_v, pmatch, pms.at[0], pmr, peer(d, d)).wait_recv()

    def hg_term(t, c):
        rows = cot_all[:, pl.ds(t, 1)].reshape(tok, feat)
        return jnp.dot(rows, w_v[:, cols(c)], preferred_element_type=f32)

    def adam(lowrank, c):
        first = decay_first * m1_v[:, cols(c)] + (1.0 - decay_first) * lowrank
        second = decay_second * m2_v[:, cols(c)] + (1.0 - decay_second) * lowrank * lowrank
        value = (first / fix_first / (jnp.sqrt(second / fix_second) + epsilon)).astype(bf16)
        dirn[pl.ds(pl.multiple_of(d * rn, rn), rn), cols(c)] = value

    def out_copies(c):
        return (
            pltpu.make_async_copy(gate_v.at[:, cols(c)], gg_out.at[:, cols(c)], out_sem.at[2 * c]),
            pltpu.make_async_copy(up_v.at[:, cols(c)], ug_out.at[:, cols(c)], out_sem.at[2 * c + 1]),
        )

    def wu_copy(c):
        slot = lax.rem(c, 2)
        return pltpu.make_async_copy(stage.at[slot], wu_out.at[:, cols(c)], wu_sem.at[slot])

    rows_step = min(256, feat)

    def phase2(s):
        @pl.when(s < CA)
        def _():
            def add(j, acc):
                return acc + jnp.dot(pall[j], hid[j, :, cols(s)], preferred_element_type=f32)

            adam(lax.fori_loop(0, n, add, jnp.zeros((rn, cw), f32)), s)

        @pl.when(jnp.logical_and(s >= CA, s < C))
        def _():
            c = s - CA
            adam(rs_take(lrb, lrs, lrr, c, lr_term(d, c)), s)

        @pl.when(s < C)
        def _():
            ag_own(dir_at, dsr, dsl, dr, s)

        ag_relay(dir_at, dsr, dsl, dr, s, C)
        rs_step(hgb, hgs, hgr, s, C, hg_term)

        c = s - lag * last

        @pl.when(c >= 0)
        def _():
            g = gate_v[:, cols(c)].astype(f32)
            u = up_v[:, cols(c)].astype(f32)
            sig = jax.nn.sigmoid(g)
            grad = rs_take(hgb, hgs, hgr, c, hg_term(d, c))
            gate_v[:, cols(c)] = (grad * u * sig * (1.0 + g * (1.0 - sig))).astype(bf16)
            up_v[:, cols(c)] = (grad * (g * sig)).astype(bf16)
            for copy in out_copies(c):
                copy.start()

            @pl.when(c >= 2)
            def _():
                wu_copy(c - 2).wait()

            slot = lax.rem(c, 2)

            def tile(i):
                rows = pl.ds(pl.multiple_of(i * rows_step, rows_step), rows_step)
                stage[slot, rows, :] = jnp.dot(
                    pmatch[rows, :], dirn[:, cols(c)], preferred_element_type=f32
                ).astype(bf16)

            each(feat // rows_step, tile)
            wu_copy(c).start()

    def both(i):
        @pl.when(i + ahead < steps1)
        def _():
            phase1(i + ahead)

        phase2(i)

    each(max(C + lag * last, steps1 - ahead), both)

    ag_drain(hid_at, hsr, hsl, hr, CA)
    rs_drain(lrb, lrs, lrr, CB)
    rs_drain(hgb, hgs, hgr, C)
    ag_drain(dir_at, dsr, dsl, dr, C)
    others(lambda q: pa_send(q).wait_send())
    others(lambda q: pb_send(q).wait_send())
    others(lambda q: c2_send(q).wait_send())

    def tail(q):
        @pl.when(jnp.logical_not(is_self(q)))
        def _():
            c1_send(q).wait_send()

            @pl.when(q < sp)
            def _():
                pz_send(q).wait_send()

    each(m, tail)

    @pl.when(o < sp)
    def _():
        others(lambda q: p3_send(q).wait_send())

    @pl.when(o == d)
    def _():
        others(lambda q: pm_send(q).wait_send())

    def finish(c):
        for copy in out_copies(c):
            copy.wait()

    each(C, finish)
    wu_copy(C - 2).wait()
    wu_copy(C - 1).wait()


def per_device(n, m, gate_pre, up_pre, cotangent, down_weight, projector, moment_first, moment_second):
    tok, ff = gate_pre.shape
    feat, rank = projector.shape
    rn = moment_first.shape[0]
    C, CA, lag = (14, 7, 1) if ff % (14 * 128) == 0 else (7, 4, 1)
    sp = min(m, rank // m // 16)
    CB = C - CA
    cw = ff // C
    dma = pltpu.SemaphoreType.DMA
    vmem = pltpu.VMEM
    return pl.pallas_call(
        functools.partial(kernel, n, m, C, CA, lag, sp),
        out_shape=(
            jax.ShapeDtypeStruct((tok, ff), bf16),
            jax.ShapeDtypeStruct((tok, ff), bf16),
            jax.ShapeDtypeStruct((feat, ff), bf16),
        ),
        in_specs=[pl.BlockSpec(memory_space=pl.ANY)] * 7,
        out_specs=[pl.BlockSpec(memory_space=pl.ANY)] * 3,
        scratch_shapes=[
            vmem((tok, ff), bf16), vmem((tok, ff), bf16), vmem(cotangent.shape, bf16),
            vmem((feat, ff), bf16), vmem((feat, rank), bf16),
            vmem((rn, ff), f32), vmem((rn, ff), f32),
            vmem((n, tok, CA * cw), bf16), vmem((tok, CB * cw), bf16), vmem((rank, ff), bf16),
            vmem((m, n, tok // m, feat), bf16), vmem((feat, rank), bf16),
            vmem((rank, tok), f32), vmem((m, rank // m, tok), f32),
            vmem((m, rank // m, tok), bf16), vmem((n, rn, tok), bf16),
            vmem((n + 1, tok, ff), bf16), vmem((n + 1, rn, CB * cw), bf16),
            vmem((2, feat, cw), bf16),
            dma((7,)), dma((2 * C,)), dma((2,)),
            dma((m,)), dma((n,)), dma((m,)), dma((m,)), dma((m,)), dma((m,)), dma((m,)), dma((m,)),
            dma((m,)), dma((n,)), dma((m,)), dma((m,)), dma((m,)), dma,
            dma((CA * n,)), dma((CA * n,)), dma((CA * n,)),
            dma((CB * n,)), dma((CB * (n + 1),)), dma((C * n,)), dma((C * (n + 1),)),
            dma((C * n,)), dma((C * n,)), dma((C * n,)),
        ],
        compiler_params=pltpu.CompilerParams(
            collective_id=0, has_side_effects=True, vmem_limit_bytes=62 * 1024 * 1024
        ),
    )(gate_pre, up_pre, cotangent, down_weight, projector, moment_first, moment_second)


def solution(mesh):
    in_specs = (
        P(("groups", "dp"), "opt"),
        P(("groups", "dp"), "opt"),
        P(("groups", "dp"), "opt"),
        P("dp", "opt"),
        P(("groups", "opt"), None),
        P(("groups", "dp"), "opt"),
        P(("groups", "dp"), "opt"),
    )
    out_specs = (P(("groups", "dp"), "opt"), P(("groups", "dp"), "opt"), P(("groups", "dp"), "opt"))
    return jax.shard_map(
        functools.partial(per_device, mesh.shape["dp"], mesh.shape["opt"]),
        mesh=mesh, in_specs=in_specs, out_specs=out_specs, check_vma=False,
    )
```
